128 devices in a mesh: group: 8 (over x, core), member: 16 (over y, z).
Axes of the slice: x: 4, y: 4, z: 4, core: 2. Of those that a mesh axis runs over, the one named last changes fastest.
Arguments:
- activations: bfloat16 [32768, 1152], P(('group', 'member')), may hold values from -6 to 6
- routes: int32 [32768, 1], P(('group', 'member')), may hold values from 0 to 127; in each aligned block of 256 rows (0 to 255, 256 to 511, ...) at most 4 rows name the same one
- centre_bias: float32 [1152], replicated, may hold values from -2 to 2
- centre_first: float32 [1152], replicated, may hold values from -600 to 600
- centre_second: float32 [1152], replicated, may hold values from 1000 to 1000000
- router: bfloat16 [128, 1152], P(('group', 'member')), may hold values from -0.1875 to 0.1875
- router_first: float32 [128, 1152], P(('group', 'member')), may hold values from -180 to 180
- router_second: float32 [128, 1152], P(('group', 'member')), may hold values from 100 to 100000
- encoder: bfloat16 [128, 1152, 512], P(('group', 'member')), may hold values from -0.1875 to 0.1875
- enc_bias: float32 [128, 512], P(('group', 'member')), may hold values from -3 to 3
- decoder: bfloat16 [128, 512, 1152], P(('group', 'member')), may hold values from -0.25 to 0.25
- encoder_first: float32 [128, 1152, 512], P(('group', 'member')), may hold values from -30 to 30
- encoder_second: float32 [128, 1152, 512], P(('group', 'member')), may hold values from 1 to 1000
- enc_bias_first: float32 [128, 512], P(('group', 'member')), may hold values from -60 to 60
- enc_bias_second: float32 [128, 512], P(('group', 'member')), may hold values from 10 to 10000
- decoder_first: float32 [128, 512, 1152], P(('group', 'member')), may hold values from -30 to 30
- decoder_second: float32 [128, 512, 1152], P(('group', 'member')), may hold values from 1 to 1000
Outputs:
- recon: bfloat16 [32768, 1152], P(('group', 'member'))
- new_centre: float32 [1152], replicated
- new_centre_first: float32 [1152], replicated
- new_centre_second: float32 [1152], replicated
- new_router: bfloat16 [128, 1152], P(('group', 'member'))
- new_router_first: float32 [128, 1152], P(('group', 'member'))
- new_router_second: float32 [128, 1152], P(('group', 'member'))
- new_encoder: bfloat16 [128, 1152, 512], P(('group', 'member'))
- new_enc_bias: float32 [128, 512], P(('group', 'member'))
- new_decoder: bfloat16 [128, 512, 1152], P(('group', 'member'))
- new_encoder_first: float32 [128, 1152, 512], P(('group', 'member'))
- new_encoder_second: float32 [128, 1152, 512], P(('group', 'member'))
- new_enc_bias_first: float32 [128, 512], P(('group', 'member'))
- new_enc_bias_second: float32 [128, 512], P(('group', 'member'))
- new_decoder_first: float32 [128, 512, 1152], P(('group', 'member'))
- new_decoder_second: float32 [128, 512, 1152], P(('group', 'member'))
The draws below stay inside these ranges and needn't reach their ends.
Inputs may be any that keep to these rules, and one draw needn't show every extreme that they name: `routes`: each row names the one expert that serves it. At most 4 rows of one device name the same expert, and in every draw some device's rows name some expert exactly 4 times.
All inputs are finite; a program needn't handle non-finite values.
Results may differ from the reference program's by a relative error of at most 0.009.
Values may be sent and summed in bfloat16 or wider, within the bound.
No kernel may reach another device: no remote copies, remote signals or barrier semaphores. Data moves between devices by JAX's collectives and lax.ppermute only.
A program may use at most 128 MiB of HBM per device.

```python
import math
import jax
import jax.numpy as jnp
import numpy as np
from jax import lax

D = 1152
LATENTS = 512
STEP = 10
TOK_DEV = 256
EXPERTS = 128
CAP = 4
TOKENS = 32768
N_GROUP = 8
N_MEMBER = 16


def block_scale(own_key, shape, cuts, least, high):
    level = 1.0
    for dim, parts in cuts:
        heights = jax.random.uniform(jax.random.fold_in(jax.random.fold_in(own_key, 6), dim), (parts,), jnp.float32, least / len(cuts), high / len(cuts))
        level = level * jnp.repeat(jnp.exp(heights), shape[dim] // parts).reshape((-1,) + (1,) * (len(shape) - 1 - dim))
    return level


def deal_out(own_key, own, number, rows, amount, top, limit, lean):
    sequence = jax.random.permutation(own_key, amount)
    packed, common = shares(amount, rows * top, limit, lean, True), shares(amount, rows * top, limit, lean, False)
    places = jnp.arange(amount)

    def named(lengths, rotation):
        used = int((lengths > 0).sum())
        fixed = max(1, used // 4)
        moved = fixed + (places - fixed + rotation * (used - fixed)) % max(1, amount - fixed)
        return jnp.zeros((amount,), jnp.int32).at[sequence[jnp.where(places < fixed, places, moved)]].set(jnp.asarray(lengths, jnp.int32))

    lengths = jnp.where(number % 4 == 0, named(packed, number // 4), named(common, number - number // 4 - 1))
    mixed = jax.random.permutation(jax.random.fold_in(own, 3), amount)
    source_of, receiver = mixed[0:amount // 2 * 2:2], mixed[1:amount // 2 * 2:2]
    margin = jnp.minimum(lengths[source_of] - 1, limit - lengths[receiver]) // 2
    margin = jnp.where((source_of == sequence[0]) | (receiver == sequence[0]) | (lengths[receiver] == 0), 0, jnp.maximum(margin, 0))
    moved = jax.random.randint(jax.random.fold_in(own, 4), (amount // 2,), 0, 1 << 20) % (margin + 1)
    lengths = lengths.at[source_of].add(-moved).at[receiver].add(moved)
    items = jnp.searchsorted(jnp.cumsum(lengths), jnp.arange(rows * top), side="right").astype(jnp.int32)
    grid = items.reshape(top, rows).T
    grid = grid[jax.random.permutation(jax.random.fold_in(own, 1), rows)]
    rotation = jax.random.randint(jax.random.fold_in(own, 2), (rows, 1), 0, top)
    return jnp.take_along_axis(grid, (jnp.arange(top)[None, :] + rotation) % top, axis=1)


def shares(number_of, total, bound, slope, full):
    weights = [(1 << 20) // math.isqrt(standing ** slope) + 1 for standing in range(1, number_of + 1)]
    largest = bound if full else min(bound, max(-(-total // number_of), total * weights[0] // sum(weights)))
    least = 1 if total - largest >= number_of - 1 else 0
    given, rest = [largest] + [least] * (number_of - 1), total - largest - least * (number_of - 1)
    while rest > 0:
        candidates = [i for i in range(1, number_of) if given[i] < largest] or [i for i in range(1, number_of) if given[i] < bound]
        whole, left = sum([weights[i] for i in candidates]), rest
        for i in candidates:
            more = min(bound - given[i], max(1, left * weights[i] // whole), rest)
            given[i] = given[i] + more
            rest = rest - more
    return np.array(given)


def scatter_about(key, extent, scale, limit, shards=(), held_as=jnp.bfloat16):
    factor_of = block_scale(key, extent, shards, -0.22, 0.18) if shards else 1.0
    array = jax.random.normal(key, extent, jnp.float32) * scale * factor_of
    return jnp.minimum(jnp.maximum(array, -limit), limit).astype(held_as)


def setup_inputs(seed: int = 0) -> dict:
    key_of = jax.random.split(jax.random.key(seed), 18)
    activations = scatter_about(key_of[0], (TOKENS, D), 1.0, 6.0, ((0, 128),))
    routes_keys = jax.random.split(jax.random.fold_in(key_of[1], 1), TOKENS // TOK_DEV)
    routes_turns = jax.random.permutation(jax.random.fold_in(key_of[1], 3), TOKENS // TOK_DEV)
    routes = jax.vmap(lambda own, number: deal_out(jax.random.fold_in(key_of[1], 2), own, number, TOK_DEV, EXPERTS, 1, CAP, 2))(routes_keys, routes_turns).reshape((TOKENS, 1))
    centre_bias = scatter_about(key_of[2], (D,), 0.3, 2.0, (), jnp.float32)
    centre_first = scatter_about(key_of[3], (D,), 100.0, 600.0, (), jnp.float32)
    centre_second = jnp.clip(jnp.exp(jax.random.uniform(key_of[4], (D,), jnp.float32, math.log(1000.0), math.log(1000000))), 1000.0, 1000000)
    router = scatter_about(key_of[5], (EXPERTS, D), D ** -0.5, 0.1875, ((0, 128),))
    router_first = scatter_about(key_of[6], (EXPERTS, D), 30.0, 180.0, ((0, 128),), jnp.float32)
    router_second = jnp.clip(jnp.exp(math.log(100000.0) - 6.9077553 * jax.random.uniform(key_of[7], (EXPERTS, D), jnp.float32) ** block_scale(key_of[7], (EXPERTS, D), ((0, 128),), -0.2, 0.2)), 100.0, 100000.0)
    encoder = scatter_about(key_of[8], (EXPERTS, D, LATENTS), D ** -0.5, 0.1875, ((0, 128),))
    enc_bias = scatter_about(key_of[9], (EXPERTS, LATENTS), 0.5, 3.0, ((0, 128),), jnp.float32)
    decoder = scatter_about(key_of[10], (EXPERTS, LATENTS, D), LATENTS ** -0.5, 0.25, ((0, 128),))
    encoder_first = scatter_about(key_of[11], (EXPERTS, D, LATENTS), 5.0, 30.0, ((0, 128),), jnp.float32)
    encoder_second = jnp.clip(jnp.exp(math.log(1000.0) - 6.9077553 * jax.random.uniform(key_of[12], (EXPERTS, D, LATENTS), jnp.float32) ** block_scale(key_of[12], (EXPERTS, D, LATENTS), ((0, 128),), -0.2, 0.2)), 1.0, 1000.0)
    enc_bias_first = scatter_about(key_of[13], (EXPERTS, LATENTS), 10.0, 60.0, ((0, 128),), jnp.float32)
    enc_bias_second = jnp.clip(jnp.exp(math.log(10000.0) - 6.9077553 * jax.random.uniform(key_of[14], (EXPERTS, LATENTS), jnp.float32) ** block_scale(key_of[14], (EXPERTS, LATENTS), ((0, 128),), -0.2, 0.2)), 10.0, 10000.0)
    decoder_first = scatter_about(key_of[15], (EXPERTS, LATENTS, D), 5.0, 30.0, ((0, 128),), jnp.float32)
    decoder_second = jnp.clip(jnp.exp(math.log(1000.0) - 6.9077553 * jax.random.uniform(key_of[16], (EXPERTS, LATENTS, D), jnp.float32) ** block_scale(key_of[16], (EXPERTS, LATENTS, D), ((0, 128),), -0.2, 0.2)), 1.0, 1000.0)
    return {"activations": activations, "routes": routes, "centre_bias": centre_bias, "centre_first": centre_first, "centre_second": centre_second, "router": router, "router_first": router_first, "router_second": router_second, "encoder": encoder, "enc_bias": enc_bias, "decoder": decoder, "encoder_first": encoder_first, "encoder_second": encoder_second, "enc_bias_first": enc_bias_first, "enc_bias_second": enc_bias_second, "decoder_first": decoder_first, "decoder_second": decoder_second}


learn_rate = 0.001
beta_one = 0.9
beta_two = 0.999
adam_eps = 1e-08
sparsity = 0.1

def adam_update(weights_in, gradient, moment_one, moment_two):
    first_new = beta_one * moment_one + (1.0 - beta_one) * gradient
    second_new = beta_two * moment_two + (1.0 - beta_two) * gradient * gradient
    first_hat = first_new / (1.0 - beta_one ** STEP)
    second_hat = second_new / (1.0 - beta_two ** STEP)
    stepped = weights_in.astype(jnp.float32) - learn_rate * first_hat / (jnp.sqrt(second_hat) + adam_eps)
    return (stepped.astype(weights_in.dtype), first_new, second_new)

def expert_pass(in_rows, live_mask, centre_bias, router_row, encoder, enc_bias, decoder):
    wide_rows = in_rows.astype(jnp.float32)
    centred = (wide_rows - centre_bias).astype(jnp.bfloat16)
    preact = jnp.dot(centred, encoder, preferred_element_type=jnp.float32) + enc_bias
    positive = jnp.maximum(preact, 0.0)
    latents = (positive * positive).astype(jnp.bfloat16)
    logits = jnp.dot(in_rows, router_row, preferred_element_type=jnp.float32)
    gating = jax.nn.sigmoid(logits)
    ungated = jnp.dot(latents, decoder, preferred_element_type=jnp.float32)
    rebuilt = centre_bias + gating[:, None] * ungated
    errors = (wide_rows - rebuilt) * live_mask[:, None]
    backward = (-gating[:, None] * errors).astype(jnp.bfloat16)
    decoder_grad = jnp.dot(latents.T, backward, preferred_element_type=jnp.float32)
    latent_grad = jnp.dot(backward, decoder.T, preferred_element_type=jnp.float32) + sparsity
    preact_grad = (latent_grad * 2.0 * positive * live_mask[:, None]).astype(jnp.bfloat16)
    encoder_grad = jnp.dot(centred.T, preact_grad, preferred_element_type=jnp.float32)
    bias_grad = lax.optimization_barrier(jnp.sum(preact_grad.astype(jnp.float32), axis=0))
    logit_grad = (-lax.optimization_barrier(jnp.sum(errors * ungated, axis=1)) * gating * (1.0 - gating)).astype(jnp.bfloat16)
    router_grad = jnp.dot(logit_grad, in_rows, preferred_element_type=jnp.float32)
    centre_part = -lax.optimization_barrier(jnp.sum(errors, axis=0)) - jnp.dot(encoder.astype(jnp.float32), bias_grad, precision=lax.Precision.HIGHEST)
    return (rebuilt.astype(jnp.bfloat16), (encoder_grad, bias_grad, decoder_grad, router_grad), centre_part)

def reference(activations, routes, centre_bias, centre_first, centre_second, router, router_first, router_second, encoder, enc_bias, decoder, encoder_first, encoder_second, enc_bias_first, enc_bias_second, decoder_first, decoder_second):
    experts = N_GROUP * N_MEMBER
    max_rows = experts * CAP
    tokens = activations.shape[0]
    route_ids = routes[:, 0]

    def per_expert(state_pair, expert_in):
        recon_all, centre_sum = state_pair
        expert_id, router_row, expert_encoder, expert_bias, expert_decoder, moments_in = expert_in
        is_mine = route_ids == expert_id
        row_index = jnp.nonzero(is_mine, size=max_rows, fill_value=0)[0].astype(jnp.int32)
        live_count = jnp.sum(is_mine.astype(jnp.int32))
        live_mask = (jnp.arange(max_rows).astype(jnp.int32) < live_count).astype(jnp.float32)
        in_rows = activations[row_index]
        rebuilt, grads, centre_part = expert_pass(in_rows, live_mask, centre_bias, router_row, expert_encoder, expert_bias, expert_decoder)
        target = jnp.where(live_mask > 0, row_index, tokens).astype(jnp.int32)
        recon_all = recon_all.at[target].set(rebuilt, mode='drop')
        router_new = adam_update(router_row, grads[3], moments_in[0], moments_in[1])
        encoder_new = adam_update(expert_encoder, grads[0], moments_in[2], moments_in[3])
        bias_new = adam_update(expert_bias, grads[1], moments_in[4], moments_in[5])
        decoder_new = adam_update(expert_decoder, grads[2], moments_in[6], moments_in[7])
        return ((recon_all, centre_sum + centre_part), (router_new, encoder_new, bias_new, decoder_new))
    zero_recon = jnp.zeros((tokens, activations.shape[1]), jnp.bfloat16)
    zero_centre = jnp.zeros((activations.shape[1],), jnp.float32)
    expert_ids = jnp.arange(experts).astype(jnp.int32)
    moments_all = (router_first, router_second, encoder_first, encoder_second, enc_bias_first, enc_bias_second, decoder_first, decoder_second)
    (recon_all, centre_grad), stacked = lax.scan(per_expert, (zero_recon, zero_centre), (expert_ids, router, encoder, enc_bias, decoder, moments_all))
    router_new, encoder_new, bias_new, decoder_new = stacked
    centre_new = adam_update(centre_bias, centre_grad, centre_first, centre_second)
    return (recon_all, centre_new[0], centre_new[1], centre_new[2], router_new[0], router_new[1], router_new[2], encoder_new[0], bias_new[0], decoder_new[0], encoder_new[1], encoder_new[2], bias_new[1], bias_new[2], decoder_new[1], decoder_new[2])
```

```python
import jax
import jax.numpy as jnp
from jax import lax
from jax.experimental import pallas as pl
from jax.experimental.pallas import tpu as pltpu
from jax.sharding import PartitionSpec as P

STEP = 10


learn_rate = 0.001
beta_one = 0.9
beta_two = 0.999
adam_eps = 1e-08
sparsity = 0.1

AXES = ("group", "member")
EMPTY_MARK = 64.0
EMPTY_LIMIT = 32.0
VMEM_LIMIT = 48 * 1024 * 1024
NT = (((1,), (1,)), ((), ()))
TN = (((0,), (0,)), ((), ()))


def adam_update(weights_in, gradient, moment_one, moment_two):
    first_new = beta_one * moment_one + (1.0 - beta_one) * gradient
    second_new = beta_two * moment_two + (1.0 - beta_two) * gradient * gradient
    first_hat = first_new * (1.0 / (1.0 - beta_one**STEP))
    second_hat = second_new * (1.0 / (1.0 - beta_two**STEP))
    stepped = weights_in.astype(jnp.float32) - learn_rate * first_hat / (
        jnp.sqrt(second_hat) + adam_eps
    )
    return (stepped.astype(weights_in.dtype), first_new, second_new)


def slot_matrix(route_row, experts, slot_cap):
    rows = route_row.shape[1]
    onehot = lax.broadcasted_iota(jnp.int32, (experts, rows), 0) == route_row
    onehot = onehot.astype(jnp.float32)
    later = lax.broadcasted_iota(jnp.int32, (rows, rows), 0) < lax.broadcasted_iota(
        jnp.int32, (rows, rows), 1
    )
    before = jnp.dot(
        onehot.astype(jnp.bfloat16),
        later.astype(jnp.float32).astype(jnp.bfloat16),
        preferred_element_type=jnp.float32,
    )
    rank = jnp.sum(before * onehot, axis=0, keepdims=True).astype(jnp.int32)
    position = route_row * slot_cap + rank
    chosen = lax.broadcasted_iota(jnp.int32, (experts * slot_cap, rows), 0) == position
    return chosen.astype(jnp.float32)


def pack_kernel(route_ref, rows_ref, packed_ref):
    experts, slot_cap, features = packed_ref.shape
    chosen = slot_matrix(route_ref[...], experts, slot_cap)
    filled = jnp.sum(chosen, axis=1, keepdims=True)
    chosen = chosen.astype(jnp.bfloat16)
    mark = (1.0 - filled) * EMPTY_MARK
    for start in range(0, features, 128):
        part = jnp.dot(
            chosen, rows_ref[:, start : start + 128], preferred_element_type=jnp.float32
        )
        if start == 0:
            part = part + mark
        packed_ref[:, :, start : start + 128] = part.astype(jnp.bfloat16).reshape(
            experts, slot_cap, 128
        )


def unpack_kernel(route_ref, returned_ref, recon_ref):
    experts, slot_cap, wide = returned_ref.shape
    features = recon_ref.shape[1]
    chosen = slot_matrix(route_ref[...], experts, slot_cap).astype(jnp.bfloat16)
    for start in range(0, features, 128):
        block = returned_ref[:, :, start : start + 128].reshape(experts * slot_cap, 128)
        recon_ref[:, start : start + 128] = lax.dot_general(
            chosen, block, TN, preferred_element_type=jnp.float32
        ).astype(jnp.bfloat16)


def expert_kernel(
    arrived_ref,
    centre_ref,
    router_ref,
    encoder_ref,
    bias_ref,
    decoder_ref,
    outgoing_ref,
    centred_ref,
    latents_ref,
    backward_ref,
    preact_grad_ref,
    bias_grad_ref,
    router_grad_ref,
    rows_ref,
    ungated_ref,
):
    sources, slot_cap, features = arrived_ref.shape
    count = sources * slot_cap
    tail = outgoing_ref.shape[2] - features
    for start in range(0, features, 128):
        rows_ref[:, start : start + 128] = arrived_ref[:, :, start : start + 128].reshape(
            count, 128
        )
    live = rows_ref[:, 0:1].astype(jnp.float32) < EMPTY_LIMIT
    first = rows_ref[:, 0:128]
    rows_ref[:, 0:128] = jnp.where(live, first.astype(jnp.float32), 0.0).astype(jnp.bfloat16)
    live_mask = live.astype(jnp.float32)
    centre = centre_ref[...]
    centred_ref[...] = (rows_ref[...].astype(jnp.float32) - centre).astype(jnp.bfloat16)
    logits = lax.dot_general(
        rows_ref[...],
        jnp.broadcast_to(router_ref[...], (8, features)),
        NT,
        preferred_element_type=jnp.float32,
    )[:, 0:1]
    gating = jax.nn.sigmoid(logits)
    preact = (
        jnp.dot(centred_ref[...], encoder_ref[...], preferred_element_type=jnp.float32)
        + bias_ref[...]
    )
    positive = jnp.maximum(preact, 0.0)
    latents_ref[...] = (positive * positive).astype(jnp.bfloat16)
    projected = jnp.zeros((count, 1), jnp.float32)
    error_sums = []
    for start in range(0, features, 128):
        block = slice(start, start + 128)
        ungated = jnp.dot(
            latents_ref[...], decoder_ref[:, block], preferred_element_type=jnp.float32
        )
        rebuilt = centre[:, block] + gating * ungated
        outgoing_ref[:, :, block] = rebuilt.astype(jnp.bfloat16).reshape(sources, slot_cap, 128)
        errors = (rows_ref[:, block].astype(jnp.float32) - rebuilt) * live_mask
        backward_ref[:, block] = (-gating * errors).astype(jnp.bfloat16)
        projected = projected + jnp.sum(errors * ungated, axis=1, keepdims=True)
        error_sums.append(jnp.sum(errors, axis=0, keepdims=True))
    latent_grad = lax.dot_general(
        backward_ref[...], decoder_ref[...], NT, preferred_element_type=jnp.float32
    )
    preact_grad = ((latent_grad + sparsity) * 2.0 * positive * live_mask).astype(jnp.bfloat16)
    preact_grad_ref[...] = preact_grad
    bias_grad = jnp.sum(preact_grad.astype(jnp.float32), axis=0, keepdims=True)
    bias_grad_ref[...] = bias_grad
    high = bias_grad.astype(jnp.bfloat16).astype(jnp.float32)
    middle = (bias_grad - high).astype(jnp.bfloat16).astype(jnp.float32)
    low = bias_grad - high - middle
    row = lax.broadcasted_iota(jnp.int32, (8, 1), 0)
    terms = jnp.where(row == 0, high, jnp.where(row == 1, middle, jnp.where(row == 2, low, 0.0)))
    passed = jnp.sum(
        lax.dot_general(
            terms.astype(jnp.bfloat16), encoder_ref[...], NT, preferred_element_type=jnp.float32
        ),
        axis=0,
        keepdims=True,
    )
    centre_part = (-jnp.concatenate(error_sums, axis=1) - passed).astype(jnp.bfloat16)
    pieces = [centre_part[:, i * tail : (i + 1) * tail] for i in range(features // tail)]
    pieces += [jnp.zeros((1, tail), jnp.bfloat16)] * (slot_cap - len(pieces))
    tail_rows = jnp.concatenate([p.astype(jnp.float32) for p in pieces], axis=0)
    outgoing_ref[:, :, features:] = jnp.broadcast_to(
        tail_rows.astype(jnp.bfloat16)[None], (sources, slot_cap, tail)
    )
    logit_grad = (-projected * gating * (1.0 - gating)).astype(jnp.bfloat16).astype(jnp.float32)
    router_grad_ref[...] = jnp.sum(
        logit_grad * rows_ref[...].astype(jnp.float32), axis=0, keepdims=True
    )


def per_device(
    activations,
    routes,
    centre_bias,
    centre_first,
    centre_second,
    router,
    router_first,
    router_second,
    encoder,
    enc_bias,
    decoder,
    encoder_first,
    encoder_second,
    enc_bias_first,
    enc_bias_second,
    decoder_first,
    decoder_second,
):
    devices = lax.axis_size("group") * lax.axis_size("member")
    row_count, features = activations.shape
    latent_count = encoder.shape[2]
    slot_cap = 2 * row_count // devices
    count = devices * slot_cap
    wide = features + features // (slot_cap - 1)
    params = pltpu.CompilerParams(vmem_limit_bytes=VMEM_LIMIT)
    route_row = routes.reshape(1, row_count)
    packed = pl.pallas_call(
        pack_kernel,
        out_shape=jax.ShapeDtypeStruct((devices, slot_cap, features), jnp.bfloat16),
        compiler_params=params,
        name="pack",
    )(route_row, activations)
    arrived = lax.all_to_all(packed, AXES, split_axis=0, concat_axis=0, tiled=True)
    outgoing, centred, latents, backward, preact_grad, bias_grad, router_grad = pl.pallas_call(
        expert_kernel,
        out_shape=(
            jax.ShapeDtypeStruct((devices, slot_cap, wide), jnp.bfloat16),
            jax.ShapeDtypeStruct((count, features), jnp.bfloat16),
            jax.ShapeDtypeStruct((count, latent_count), jnp.bfloat16),
            jax.ShapeDtypeStruct((count, features), jnp.bfloat16),
            jax.ShapeDtypeStruct((count, latent_count), jnp.bfloat16),
            jax.ShapeDtypeStruct((1, latent_count), jnp.float32),
            jax.ShapeDtypeStruct((1, features), jnp.float32),
        ),
        scratch_shapes=[
            pltpu.VMEM((count, features), jnp.bfloat16),
            pltpu.VMEM((8, 128), jnp.float32),
        ],
        compiler_params=params,
        name="expert",
    )(arrived, centre_bias[None], router, encoder[0], enc_bias, decoder[0])
    returned = lax.all_to_all(outgoing, AXES, split_axis=0, concat_axis=0, tiled=True)
    decoder_grad = lax.dot_general(latents, backward, TN, preferred_element_type=jnp.float32)
    encoder_grad = lax.dot_general(centred, preact_grad, TN, preferred_element_type=jnp.float32)
    router_new = adam_update(router, router_grad, router_first, router_second)
    encoder_new = adam_update(encoder[0], encoder_grad, encoder_first[0], encoder_second[0])
    bias_new = adam_update(enc_bias, bias_grad, enc_bias_first, enc_bias_second)
    decoder_new = adam_update(decoder[0], decoder_grad, decoder_first[0], decoder_second[0])
    recon = pl.pallas_call(
        unpack_kernel,
        out_shape=jax.ShapeDtypeStruct((row_count, features), jnp.bfloat16),
        compiler_params=params,
        name="unpack",
    )(route_row, returned)
    centre_total = jnp.sum(
        returned[:, : slot_cap - 1, features:].astype(jnp.float32), axis=0
    ).reshape(features)
    centre_new = adam_update(centre_bias, centre_total, centre_first, centre_second)
    return (
        recon,
        centre_new[0],
        centre_new[1],
        centre_new[2],
        router_new[0],
        router_new[1],
        router_new[2],
        encoder_new[0][None],
        bias_new[0],
        decoder_new[0][None],
        encoder_new[1][None],
        encoder_new[2][None],
        bias_new[1],
        bias_new[2],
        decoder_new[1][None],
        decoder_new[2][None],
    )


def solution(mesh):
    whole, rows, blocks = P(), P(AXES, None), P(AXES, None, None)
    return jax.shard_map(
        per_device,
        mesh=mesh,
        in_specs=(
            rows, rows, whole, whole, whole, rows, rows, rows, blocks, rows, blocks,
            blocks, blocks, rows, rows, blocks, blocks,
        ),
        out_specs=(
            rows, whole, whole, whole, rows, rows, rows, blocks, rows, blocks,
            blocks, blocks, rows, rows, blocks, blocks,
        ),
        check_vma=False,
    )
```

```python
import jax
import jax.numpy as jnp
from jax import lax
from jax.experimental import pallas as pl
from jax.experimental.pallas import tpu as pltpu
from jax.sharding import PartitionSpec as P

STEP = 10


learn_rate = 0.001
beta_one = 0.9
beta_two = 0.999
adam_eps = 1e-08
sparsity = 0.1

AXES = ("group", "member")
EMPTY_MARK = 64.0
EMPTY_LIMIT = 32.0
VMEM_LIMIT = 20 * 1024 * 1024
STEP_LIMIT = 36 * 1024 * 1024
NT = (((1,), (1,)), ((), ()))
TN = (((0,), (0,)), ((), ()))


def adam_update(weights_in, gradient, moment_one, moment_two):
    first_new = beta_one * moment_one + (1.0 - beta_one) * gradient
    second_new = beta_two * moment_two + (1.0 - beta_two) * gradient * gradient
    first_hat = first_new * (1.0 / (1.0 - beta_one**STEP))
    second_hat = second_new * (1.0 / (1.0 - beta_two**STEP))
    stepped = weights_in.astype(jnp.float32) - learn_rate * first_hat / (
        jnp.sqrt(second_hat) + adam_eps
    )
    return (stepped.astype(weights_in.dtype), first_new, second_new)


def slot_matrix(route_row, experts, slot_cap):
    rows = route_row.shape[1]
    onehot = lax.broadcasted_iota(jnp.int32, (experts, rows), 0) == route_row
    onehot = onehot.astype(jnp.float32)
    later = lax.broadcasted_iota(jnp.int32, (rows, rows), 0) < lax.broadcasted_iota(
        jnp.int32, (rows, rows), 1
    )
    before = jnp.dot(
        onehot.astype(jnp.bfloat16),
        later.astype(jnp.float32).astype(jnp.bfloat16),
        preferred_element_type=jnp.float32,
    )
    rank = jnp.sum(before * onehot, axis=0, keepdims=True).astype(jnp.int32)
    position = route_row * slot_cap + rank
    chosen = lax.broadcasted_iota(jnp.int32, (experts * slot_cap, rows), 0) == position
    return chosen.astype(jnp.float32)


def taken_kernel(route_ref, taken_ref):
    rows, slots = taken_ref.shape
    experts = lax.axis_size("group") * lax.axis_size("member")
    taken_ref[...] = slot_matrix(route_ref[...], experts, slots // experts).T.astype(jnp.bfloat16)


def pack_kernel(route_ref, rows_ref, packed_ref, route_vmem, rows_vmem, packed_vmem, sems):
    experts, slot_cap, features = packed_ref.shape
    fetch_route = pltpu.make_async_copy(route_ref, route_vmem, sems.at[1])
    fetch_route.start()
    fetch = pltpu.make_async_copy(rows_ref, rows_vmem, sems.at[0])
    fetch.start()
    fetch_route.wait()
    chosen = slot_matrix(route_vmem[...], experts, slot_cap)
    mark = (1.0 - jnp.sum(chosen, axis=1, keepdims=True)) * EMPTY_MARK
    chosen = chosen.astype(jnp.bfloat16)
    fetch.wait()
    copies = []
    for i, (start, width) in enumerate(column_blocks(features)):
        block = slice(start, start + width)
        part = jnp.dot(chosen, rows_vmem[:, block], preferred_element_type=jnp.float32)
        if start == 0:
            part = part + mark
        packed_vmem[:, :, block] = part.astype(jnp.bfloat16).reshape(experts, slot_cap, width)
        copies.append(
            pltpu.make_async_copy(
                packed_vmem.at[:, :, block], packed_ref.at[:, :, block], sems.at[1 + i]
            )
        )
        copies[-1].start()
    for copy in copies:
        copy.wait()


def unpack_kernel(
    taken_ref, returned_ref, centre_ref, first_ref, second_ref,
    recon_ref, new_centre_ref, new_first_ref, new_second_ref,
):
    experts, slot_cap, wide = returned_ref.shape
    features = recon_ref.shape[1]
    tail = wide - features
    taken = taken_ref[...]
    for start, width in column_blocks(features):
        block = slice(start, start + width)
        returned = returned_ref[:, :, block].reshape(experts * slot_cap, width)
        recon_ref[:, block] = jnp.dot(
            taken, returned, preferred_element_type=jnp.float32
        ).astype(jnp.bfloat16)
    total = jnp.sum(returned_ref[:, :, features:].astype(jnp.float32), axis=0)
    for i in range(features // tail):
        block = slice(i * tail, (i + 1) * tail)
        updated = adam_update(
            centre_ref[:, block], total[i : i + 1], first_ref[:, block], second_ref[:, block]
        )
        for value, target in zip(updated, (new_centre_ref, new_first_ref, new_second_ref)):
            target[block] = value.reshape(tail)


def column_blocks(features, width=256):
    return [(start, min(width, features - start)) for start in range(0, features, width)]


def expert_kernel(
    arrived_ref,
    centre_ref,
    router_ref,
    encoder_ref,
    bias_ref,
    decoder_hbm,
    outgoing_hbm,
    rows_hbm,
    latents_hbm,
    backward_hbm,
    preact_grad_hbm,
    bias_grad_ref,
    logit_grad_ref,
    rows_ref,
    latents_ref,
    backward_ref,
    preact_grad_ref,
    centred_ref,
    decoder_ref,
    outgoing_ref,
    positive_ref,
    sems,
    side_sems,
):
    sources, slot_cap, features = arrived_ref.shape
    count = sources * slot_cap
    tail = outgoing_ref.shape[2] - features
    fetch = pltpu.make_async_copy(decoder_hbm, decoder_ref, sems.at[0])
    fetch.start()
    copies = []

    def write_out(source, target, sem):
        copies.append(pltpu.make_async_copy(source, target, sem))
        copies[-1].start()

    centre = centre_ref[...]
    live = None
    for start, width in column_blocks(features):
        block = slice(start, start + width)
        wide_rows = arrived_ref[:, :, block].reshape(count, width)
        if live is None:
            live = wide_rows[:, 0:1].astype(jnp.float32) < EMPTY_LIMIT
            wide_rows = jnp.where(live, wide_rows.astype(jnp.float32), 0.0).astype(jnp.bfloat16)
        rows_ref[:, block] = wide_rows
        centred_ref[:, block] = (wide_rows.astype(jnp.float32) - centre[:, block]).astype(
            jnp.bfloat16
        )
    write_out(rows_ref, rows_hbm, side_sems.at[0])
    live_mask = live.astype(jnp.float32)
    logits = lax.dot_general(
        rows_ref[...],
        jnp.broadcast_to(router_ref[...], (8, features)),
        NT,
        preferred_element_type=jnp.float32,
    )[:, 0:1]
    gating = jax.nn.sigmoid(logits)
    for start, width in column_blocks(encoder_ref.shape[1]):
        block = slice(start, start + width)
        preact = (
            jnp.dot(centred_ref[...], encoder_ref[:, block], preferred_element_type=jnp.float32)
            + bias_ref[:, block]
        )
        positive = jnp.maximum(preact, 0.0)
        positive_ref[:, block] = positive * live_mask
        latents_ref[:, block] = (positive * positive).astype(jnp.bfloat16)
    write_out(latents_ref, latents_hbm, side_sems.at[1])
    fetch.wait()
    projected = jnp.zeros((count, 1), jnp.float32)
    error_sums = []
    for i, (start, width) in enumerate(column_blocks(features)):
        block = slice(start, start + width)
        ungated = jnp.dot(
            latents_ref[...], decoder_ref[:, block], preferred_element_type=jnp.float32
        )
        rebuilt = centre[:, block] + gating * ungated
        outgoing_ref[:, :, block] = rebuilt.astype(jnp.bfloat16).reshape(sources, slot_cap, width)
        write_out(outgoing_ref.at[:, :, block], outgoing_hbm.at[:, :, block], sems.at[1 + i])
        errors = (rows_ref[:, block].astype(jnp.float32) - rebuilt) * live_mask
        backward_ref[:, block] = (-gating * errors).astype(jnp.bfloat16)
        projected = projected + jnp.sum(errors * ungated, axis=1, keepdims=True)
        error_sums.append(jnp.sum(errors, axis=0, keepdims=True))
    write_out(backward_ref, backward_hbm, side_sems.at[2])
    logit_grad_ref[...] = -projected * gating * (1.0 - gating)
    bias_grads = []
    for start, width in column_blocks(encoder_ref.shape[1]):
        block = slice(start, start + width)
        latent_grad = lax.dot_general(
            backward_ref[...], decoder_ref[block, :], NT, preferred_element_type=jnp.float32
        )
        preact_grad = ((latent_grad + sparsity) * 2.0 * positive_ref[:, block]).astype(jnp.bfloat16)
        preact_grad_ref[:, block] = preact_grad
        bias_grads.append(jnp.sum(preact_grad.astype(jnp.float32), axis=0, keepdims=True))
    write_out(preact_grad_ref, preact_grad_hbm, side_sems.at[3])
    bias_grad = jnp.concatenate(bias_grads, axis=1)
    bias_grad_ref[...] = bias_grad
    high = bias_grad.astype(jnp.bfloat16).astype(jnp.float32)
    middle = (bias_grad - high).astype(jnp.bfloat16).astype(jnp.float32)
    low = bias_grad - high - middle
    row = lax.broadcasted_iota(jnp.int32, (8, 1), 0)
    terms = jnp.where(row == 0, high, jnp.where(row == 1, middle, jnp.where(row == 2, low, 0.0)))
    passed = jnp.sum(
        lax.dot_general(
            terms.astype(jnp.bfloat16), encoder_ref[...], NT, preferred_element_type=jnp.float32
        ),
        axis=0,
        keepdims=True,
    )
    centre_part = -jnp.concatenate(error_sums, axis=1) - passed
    pieces = [centre_part[:, i * tail : (i + 1) * tail] for i in range(features // tail)]
    pieces += [jnp.zeros((1, tail), jnp.float32)] * (slot_cap - len(pieces))
    outgoing_ref[:, :, features:] = jnp.broadcast_to(
        jnp.concatenate(pieces, axis=0).astype(jnp.bfloat16)[None], (sources, slot_cap, tail)
    )
    write_out(outgoing_ref.at[:, :, features:], outgoing_hbm.at[:, :, features:], sems.at[0])
    for copy in copies:
        copy.wait()


def step_kernel(centre_ref, *refs):
    sources, targets = refs[:10], refs[10:16]
    arrived, made, (in_sems, out_sems) = refs[16:26], refs[26:32], refs[32:]
    rows, preact_grad, latents, backward = arrived[:4]
    plan = (
        (rows, preact_grad, (0, 1), (4, 5, 6), (0, 1, 2)),
        (latents, backward, (2, 3), (7, 8, 9), (3, 4, 5)),
    )
    fetches, started = [], 0
    for left, right, whole, state, _ in plan:
        waits = []
        for i in whole:
            waits.append(pltpu.make_async_copy(sources[i], arrived[i], in_sems.at[started]))
            started += 1
        for start, width in column_blocks(left.shape[1]):
            block = slice(start, start + width)
            for i in state:
                waits.append(
                    pltpu.make_async_copy(
                        sources[i].at[block, :], arrived[i].at[block, :], in_sems.at[started]
                    )
                )
                started += 1
            fetches.append(waits)
            waits = []
    for waits in fetches:
        for copy in waits:
            copy.start()
    copies = []
    fetched = iter(fetches)
    for left, right, _, state, made_here in plan:
        weights, first, second = (arrived[i] for i in state)
        for start, width in column_blocks(left.shape[1]):
            block = slice(start, start + width)
            for copy in next(fetched):
                copy.wait()
            turned = left[:, block]
            if left is rows:
                turned = (turned.astype(jnp.float32) - centre_ref[:, block]).astype(jnp.bfloat16)
            gradient = lax.dot_general(turned, right[...], TN, preferred_element_type=jnp.float32)
            updated = adam_update(weights[block, :], gradient, first[block, :], second[block, :])
            for value, i in zip(updated, made_here):
                made[i][block, :] = value
                copies.append(
                    pltpu.make_async_copy(
                        made[i].at[block, :], targets[i].at[block, :], out_sems.at[len(copies)]
                    )
                )
                copies[-1].start()
    for copy in copies:
        copy.wait()


def in_hbm(*arrays):
    return [pltpu.with_memory_space_constraint(array, pltpu.HBM) for array in arrays]


def per_device(
    activations,
    routes,
    centre_bias,
    centre_first,
    centre_second,
    router,
    router_first,
    router_second,
    encoder,
    enc_bias,
    decoder,
    encoder_first,
    encoder_second,
    enc_bias_first,
    enc_bias_second,
    decoder_first,
    decoder_second,
):
    devices = lax.axis_size("group") * lax.axis_size("member")
    row_count, features = activations.shape
    latent_count = encoder.shape[2]
    slot_cap = 2 * row_count // devices
    count = devices * slot_cap
    wide = features + features // (slot_cap - 1)
    params = pltpu.CompilerParams(vmem_limit_bytes=VMEM_LIMIT)
    hbm = pl.BlockSpec(memory_space=pltpu.HBM)
    local = pl.BlockSpec(memory_space=pltpu.VMEM)
    copies = len(column_blocks(features)) + 1
    route_row = routes.reshape(1, row_count)
    packed = pl.pallas_call(
        pack_kernel,
        in_specs=[hbm, hbm],
        out_specs=hbm,
        out_shape=pltpu.HBM((devices, slot_cap, features), jnp.bfloat16),
        scratch_shapes=[
            pltpu.VMEM((1, row_count), jnp.int32),
            pltpu.VMEM((row_count, features), jnp.bfloat16),
            pltpu.VMEM((devices, slot_cap, features), jnp.bfloat16),
            pltpu.SemaphoreType.DMA((copies,)),
        ],
        compiler_params=pltpu.CompilerParams(vmem_limit_bytes=VMEM_LIMIT),
        name="pack",
    )(*in_hbm(route_row, activations))
    arrived = lax.all_to_all(packed, AXES, split_axis=0, concat_axis=0, tiled=True)
    (outgoing, rows, latents, backward, preact_grad, bias_grad, logit_grad) = pl.pallas_call(
        expert_kernel,
        in_specs=[local, local, local, local, local, hbm],
        out_specs=(hbm,) * 5 + (local,) * 2,
        out_shape=(
            pltpu.HBM((devices, slot_cap, wide), jnp.bfloat16),
            pltpu.HBM((count, features), jnp.bfloat16),
            pltpu.HBM((count, latent_count), jnp.bfloat16),
            pltpu.HBM((count, features), jnp.bfloat16),
            pltpu.HBM((count, latent_count), jnp.bfloat16),
            jax.ShapeDtypeStruct((1, latent_count), jnp.float32),
            jax.ShapeDtypeStruct((count, 1), jnp.float32),
        ),
        scratch_shapes=[
            pltpu.VMEM((count, features), jnp.bfloat16),
            pltpu.VMEM((count, latent_count), jnp.bfloat16),
            pltpu.VMEM((count, features), jnp.bfloat16),
            pltpu.VMEM((count, latent_count), jnp.bfloat16),
            pltpu.VMEM((count, features), jnp.bfloat16),
            pltpu.VMEM((latent_count, features), jnp.bfloat16),
            pltpu.VMEM((devices, slot_cap, wide), jnp.bfloat16),
            pltpu.VMEM((count, latent_count), jnp.float32),
            pltpu.SemaphoreType.DMA((copies,)),
            pltpu.SemaphoreType.DMA((4,)),
        ],
        compiler_params=pltpu.CompilerParams(vmem_limit_bytes=VMEM_LIMIT),
        name="expert",
    )(
        arrived,
        centre_bias[None],
        router,
        encoder[0],
        enc_bias,
        *in_hbm(decoder[0]),
    )
    returned = lax.all_to_all(outgoing, AXES, split_axis=0, concat_axis=0, tiled=True)
    router_grad = jnp.dot(
        logit_grad.astype(jnp.bfloat16).T, rows, preferred_element_type=jnp.float32
    )
    router_new = adam_update(router, router_grad, router_first, router_second)
    bias_new = adam_update(enc_bias, bias_grad, enc_bias_first, enc_bias_second)
    matrices = (
        encoder[0], encoder_first[0], encoder_second[0],
        decoder[0], decoder_first[0], decoder_second[0],
    )
    operands = (rows, preact_grad, latents, backward) + matrices
    pieces = 3 * (len(column_blocks(features)) + len(column_blocks(latent_count)))
    stepped = pl.pallas_call(
        step_kernel,
        in_specs=[local] + [hbm] * 10,
        out_specs=(hbm,) * 6,
        out_shape=tuple(pltpu.HBM(array.shape, array.dtype) for array in matrices),
        scratch_shapes=[pltpu.VMEM(array.shape, array.dtype) for array in operands + matrices]
        + [pltpu.SemaphoreType.DMA((pieces + 4,)), pltpu.SemaphoreType.DMA((pieces,))],
        compiler_params=pltpu.CompilerParams(vmem_limit_bytes=STEP_LIMIT),
        cost_estimate=pl.CostEstimate(
            flops=4 * count * features * latent_count,
            bytes_accessed=20 * features * latent_count,
            transcendentals=0,
        ),
        name="step",
    )(centre_bias[None], *in_hbm(*operands))
    encoder_new, decoder_new = stepped[:3], stepped[3:]
    taken = pl.pallas_call(
        taken_kernel,
        out_shape=jax.ShapeDtypeStruct((row_count, count), jnp.bfloat16),
        compiler_params=pltpu.CompilerParams(vmem_limit_bytes=VMEM_LIMIT),
        name="taken",
    )(route_row)
    recon, *centre_new = pl.pallas_call(
        unpack_kernel,
        out_shape=(jax.ShapeDtypeStruct((row_count, features), jnp.bfloat16),)
        + (jax.ShapeDtypeStruct((features,), jnp.float32),) * 3,
        compiler_params=params,
        name="unpack",
    )(taken, returned, centre_bias[None], centre_first[None], centre_second[None])
    return (
        recon,
        centre_new[0],
        centre_new[1],
        centre_new[2],
        router_new[0],
        router_new[1],
        router_new[2],
        encoder_new[0][None],
        bias_new[0],
        decoder_new[0][None],
        encoder_new[1][None],
        encoder_new[2][None],
        bias_new[1],
        bias_new[2],
        decoder_new[1][None],
        decoder_new[2][None],
    )


def solution(mesh):
    whole, rows, blocks = P(), P(AXES, None), P(AXES, None, None)
    return jax.shard_map(
        per_device,
        mesh=mesh,
        in_specs=(
            rows, rows, whole, whole, whole, rows, rows, rows, blocks, rows, blocks,
            blocks, blocks, rows, rows, blocks, blocks,
        ),
        out_specs=(
            rows, whole, whole, whole, rows, rows, rows, blocks, rows, blocks,
            blocks, blocks, rows, rows, blocks, blocks,
        ),
        check_vma=False,
    )
```

```python
import jax
import jax.numpy as jnp
from jax import lax
from jax.experimental import pallas as pl
from jax.experimental.pallas import tpu as pltpu
from jax.sharding import PartitionSpec as P

STEP = 10


learn_rate = 0.001
beta_one = 0.9
beta_two = 0.999
adam_eps = 1e-08
sparsity = 0.1

AXES = ("group", "member")
EMPTY_MARK = 64.0
EMPTY_LIMIT = 32.0
VMEM_LIMIT = 20 * 1024 * 1024
STEP_LIMIT = 36 * 1024 * 1024
PARTS = 1
TAIL_COPIES = 4
NT = (((1,), (1,)), ((), ()))
TN = (((0,), (0,)), ((), ()))


def adam_update(weights_in, gradient, moment_one, moment_two):
    first_new = beta_one * moment_one + (1.0 - beta_one) * gradient
    second_new = beta_two * moment_two + (1.0 - beta_two) * gradient * gradient
    first_hat = first_new * (1.0 / (1.0 - beta_one**STEP))
    second_hat = second_new * (1.0 / (1.0 - beta_two**STEP))
    stepped = weights_in.astype(jnp.float32) - learn_rate * first_hat / (
        jnp.sqrt(second_hat) + adam_eps
    )
    return (stepped.astype(weights_in.dtype), first_new, second_new)


def slot_matrix(route_row, experts, slot_cap):
    rows = route_row.shape[1]
    onehot = lax.broadcasted_iota(jnp.int32, (experts, rows), 0) == route_row
    onehot = onehot.astype(jnp.float32)
    later = lax.broadcasted_iota(jnp.int32, (rows, rows), 0) < lax.broadcasted_iota(
        jnp.int32, (rows, rows), 1
    )
    before = jnp.dot(
        onehot.astype(jnp.bfloat16),
        later.astype(jnp.float32).astype(jnp.bfloat16),
        preferred_element_type=jnp.float32,
    )
    rank = jnp.sum(before * onehot, axis=0, keepdims=True).astype(jnp.int32)
    position = route_row * slot_cap + rank
    chosen = lax.broadcasted_iota(jnp.int32, (experts * slot_cap, rows), 0) == position
    return chosen.astype(jnp.float32)


def taken_kernel(route_ref, taken_ref):
    rows, slots = taken_ref.shape
    experts = lax.axis_size("group") * lax.axis_size("member")
    taken_ref[...] = slot_matrix(route_ref[...], experts, slots // experts).T.astype(jnp.bfloat16)


def pack_kernel(route_ref, rows_ref, packed_ref, route_vmem, rows_vmem, packed_vmem, sems):
    experts, slot_cap, features = packed_ref.shape
    fetch_route = pltpu.make_async_copy(route_ref, route_vmem, sems.at[1])
    fetch_route.start()
    fetch = pltpu.make_async_copy(rows_ref, rows_vmem, sems.at[0])
    fetch.start()
    fetch_route.wait()
    chosen = slot_matrix(route_vmem[...], experts, slot_cap)
    mark = (1.0 - jnp.sum(chosen, axis=1, keepdims=True)) * EMPTY_MARK
    chosen = chosen.astype(jnp.bfloat16)
    fetch.wait()
    copies = []
    for i, (start, width) in enumerate(column_blocks(features)):
        block = slice(start, start + width)
        part = jnp.dot(chosen, rows_vmem[:, block], preferred_element_type=jnp.float32)
        if start == 0:
            part = part + mark
        packed_vmem[:, :, block] = part.astype(jnp.bfloat16).reshape(experts, slot_cap, width)
        copies.append(
            pltpu.make_async_copy(
                packed_vmem.at[:, :, block], packed_ref.at[:, :, block], sems.at[1 + i]
            )
        )
        copies[-1].start()
    for copy in copies:
        copy.wait()


def unpack_kernel(
    taken_ref, returned_ref, centre_ref, first_ref, second_ref,
    recon_ref, new_centre_ref, new_first_ref, new_second_ref,
):
    experts, slot_cap, wide = returned_ref.shape
    features = recon_ref.shape[1]
    tail = wide - features
    taken = taken_ref[...]
    for start, width in column_blocks(features):
        block = slice(start, start + width)
        returned = returned_ref[:, :, block].reshape(experts * slot_cap, width)
        recon_ref[:, block] = jnp.dot(
            taken, returned, preferred_element_type=jnp.float32
        ).astype(jnp.bfloat16)
    total = jnp.sum(returned_ref[:, :, features:].astype(jnp.float32), axis=0)
    for i in range(features // tail):
        block = slice(i * tail, (i + 1) * tail)
        updated = adam_update(
            centre_ref[:, block], total[i : i + 1], first_ref[:, block], second_ref[:, block]
        )
        for value, target in zip(updated, (new_centre_ref, new_first_ref, new_second_ref)):
            target[block] = value.reshape(tail)


def column_blocks(features, width=256):
    return [(start, min(width, features - start)) for start in range(0, features, width)]


def expert_kernel(
    arrived_ref,
    centre_ref,
    router_ref,
    encoder_ref,
    bias_ref,
    decoder_hbm,
    outgoing_hbm,
    rows_hbm,
    latents_hbm,
    backward_hbm,
    preact_grad_hbm,
    bias_grad_ref,
    logit_grad_ref,
    rows_ref,
    latents_ref,
    backward_ref,
    preact_grad_ref,
    centred_ref,
    decoder_ref,
    outgoing_ref,
    positive_ref,
    sems,
    side_sems,
):
    sources, slot_cap, features = arrived_ref.shape
    count = sources * slot_cap
    tail = outgoing_ref.shape[2] - features
    fetch = pltpu.make_async_copy(decoder_hbm, decoder_ref, sems.at[0])
    fetch.start()
    copies = []

    def write_out(source, target, sem):
        copies.append(pltpu.make_async_copy(source, target, sem))
        copies[-1].start()

    centre = centre_ref[...]
    router_rows = jnp.broadcast_to(router_ref[...], (8, features))
    blocks = [slice(start, start + width) for start, width in column_blocks(features)]
    latent_blocks = [
        slice(start, start + width) for start, width in column_blocks(encoder_ref.shape[1])
    ]
    error_sums = [jnp.zeros((1, features), jnp.float32)]
    bias_grads = [jnp.zeros((1, encoder_ref.shape[1]), jnp.float32)]
    held = []
    for part in range(PARTS):
        rows = slice(part * count // PARTS, (part + 1) * count // PARTS)
        owners = slice(part * sources // PARTS, (part + 1) * sources // PARTS)
        live = None
        for block in blocks:
            wide_rows = arrived_ref[owners, :, block].reshape(
                count // PARTS, block.stop - block.start
            )
            if live is None:
                live = wide_rows[:, 0:1].astype(jnp.float32) < EMPTY_LIMIT
                wide_rows = jnp.where(live, wide_rows.astype(jnp.float32), 0.0).astype(jnp.bfloat16)
            rows_ref[rows, block] = wide_rows
            centred_ref[rows, block] = (wide_rows.astype(jnp.float32) - centre[:, block]).astype(
                jnp.bfloat16
            )
        live_mask = live.astype(jnp.float32)
        logits = lax.dot_general(
            rows_ref[rows, :], router_rows, NT, preferred_element_type=jnp.float32
        )[:, 0:1]
        gating = jax.nn.sigmoid(logits)
        for block in latent_blocks:
            preact = (
                jnp.dot(
                    centred_ref[rows, :], encoder_ref[:, block], preferred_element_type=jnp.float32
                )
                + bias_ref[:, block]
            )
            positive = jnp.maximum(preact, 0.0)
            positive_ref[rows, block] = positive * live_mask
            latents_ref[rows, block] = (positive * positive).astype(jnp.bfloat16)
        held.append((rows, owners, live_mask, gating))
    write_out(rows_ref, rows_hbm, side_sems.at[0])
    write_out(latents_ref, latents_hbm, side_sems.at[1])
    fetch.wait()
    for part, (rows, owners, live_mask, gating) in enumerate(held):
        projected = jnp.zeros((count // PARTS, 1), jnp.float32)
        sums = []
        for block in blocks:
            ungated = jnp.dot(
                latents_ref[rows, :], decoder_ref[:, block], preferred_element_type=jnp.float32
            )
            rebuilt = centre[:, block] + gating * ungated
            outgoing_ref[owners, :, block] = rebuilt.astype(jnp.bfloat16).reshape(
                sources // PARTS, slot_cap, block.stop - block.start
            )
            errors = (rows_ref[rows, block].astype(jnp.float32) - rebuilt) * live_mask
            backward_ref[rows, block] = (-gating * errors).astype(jnp.bfloat16)
            projected = projected + jnp.sum(errors * ungated, axis=1, keepdims=True)
            sums.append(jnp.sum(errors, axis=0, keepdims=True))
        error_sums.append(jnp.concatenate(sums, axis=1))
        logit_grad_ref[rows, :] = -projected * gating * (1.0 - gating)
        sums = []
        for block in latent_blocks:
            latent_grad = lax.dot_general(
                backward_ref[rows, :], decoder_ref[block, :], NT, preferred_element_type=jnp.float32
            )
            preact_grad = ((latent_grad + sparsity) * 2.0 * positive_ref[rows, block]).astype(
                jnp.bfloat16
            )
            preact_grad_ref[rows, block] = preact_grad
            sums.append(jnp.sum(preact_grad.astype(jnp.float32), axis=0, keepdims=True))
        bias_grads.append(jnp.concatenate(sums, axis=1))
        write_out(
            outgoing_ref.at[owners, :, 0:features],
            outgoing_hbm.at[owners, :, 0:features],
            sems.at[1 + part],
        )
    write_out(backward_ref, backward_hbm, side_sems.at[2])
    write_out(preact_grad_ref, preact_grad_hbm, side_sems.at[3])
    bias_grad = sum(bias_grads)
    bias_grad_ref[...] = bias_grad
    high = bias_grad.astype(jnp.bfloat16).astype(jnp.float32)
    middle = (bias_grad - high).astype(jnp.bfloat16).astype(jnp.float32)
    low = bias_grad - high - middle
    row = lax.broadcasted_iota(jnp.int32, (8, 1), 0)
    terms = jnp.where(row == 0, high, jnp.where(row == 1, middle, jnp.where(row == 2, low, 0.0)))
    passed = jnp.sum(
        lax.dot_general(
            terms.astype(jnp.bfloat16), encoder_ref[...], NT, preferred_element_type=jnp.float32
        ),
        axis=0,
        keepdims=True,
    )
    centre_part = -sum(error_sums) - passed
    pieces = [centre_part[:, i * tail : (i + 1) * tail] for i in range(features // tail)]
    pieces += [jnp.zeros((1, tail), jnp.float32)] * (slot_cap - len(pieces))
    outgoing_ref[:, :, features:] = jnp.broadcast_to(
        jnp.concatenate(pieces, axis=0).astype(jnp.bfloat16)[None], (sources, slot_cap, tail)
    )
    for i in range(TAIL_COPIES):
        owners = slice(i * sources // TAIL_COPIES, (i + 1) * sources // TAIL_COPIES)
        write_out(
            outgoing_ref.at[owners, :, features:],
            outgoing_hbm.at[owners, :, features:],
            sems.at[1 + PARTS + i],
        )
    for copy in copies:
        copy.wait()


def step_kernel(centre_ref, *refs):
    sources, targets = refs[:10], refs[10:16]
    arrived, made, (in_sems, out_sems) = refs[16:26], refs[26:32], refs[32:]
    rows, preact_grad, latents, backward = arrived[:4]
    plan = (
        (rows, preact_grad, (0, 1), (4, 5, 6), (0, 1, 2)),
        (latents, backward, (2, 3), (7, 8, 9), (3, 4, 5)),
    )
    fetches, started = [], 0
    for left, right, whole, state, _ in plan:
        waits = []
        for i in whole:
            waits.append(pltpu.make_async_copy(sources[i], arrived[i], in_sems.at[started]))
            started += 1
        for start, width in column_blocks(left.shape[1]):
            block = slice(start, start + width)
            for i in state:
                waits.append(
                    pltpu.make_async_copy(
                        sources[i].at[block, :], arrived[i].at[block, :], in_sems.at[started]
                    )
                )
                started += 1
            fetches.append(waits)
            waits = []
    for waits in fetches:
        for copy in waits:
            copy.start()
    copies = []
    fetched = iter(fetches)
    for left, right, _, state, made_here in plan:
        weights, first, second = (arrived[i] for i in state)
        for start, width in column_blocks(left.shape[1]):
            block = slice(start, start + width)
            for copy in next(fetched):
                copy.wait()
            turned = left[:, block]
            if left is rows:
                turned = (turned.astype(jnp.float32) - centre_ref[:, block]).astype(jnp.bfloat16)
            gradient = lax.dot_general(turned, right[...], TN, preferred_element_type=jnp.float32)
            updated = adam_update(weights[block, :], gradient, first[block, :], second[block, :])
            for value, i in zip(updated, made_here):
                made[i][block, :] = value
                copies.append(
                    pltpu.make_async_copy(
                        made[i].at[block, :], targets[i].at[block, :], out_sems.at[len(copies)]
                    )
                )
                copies[-1].start()
    for copy in copies:
        copy.wait()


def in_hbm(*arrays):
    return [pltpu.with_memory_space_constraint(array, pltpu.HBM) for array in arrays]


def per_device(
    activations,
    routes,
    centre_bias,
    centre_first,
    centre_second,
    router,
    router_first,
    router_second,
    encoder,
    enc_bias,
    decoder,
    encoder_first,
    encoder_second,
    enc_bias_first,
    enc_bias_second,
    decoder_first,
    decoder_second,
):
    devices = lax.axis_size("group") * lax.axis_size("member")
    row_count, features = activations.shape
    latent_count = encoder.shape[2]
    slot_cap = 2 * row_count // devices
    count = devices * slot_cap
    wide = features + features // (slot_cap - 1)
    params = pltpu.CompilerParams(vmem_limit_bytes=VMEM_LIMIT)
    hbm = pl.BlockSpec(memory_space=pltpu.HBM)
    local = pl.BlockSpec(memory_space=pltpu.VMEM)
    copies = len(column_blocks(features)) + 1
    route_row = routes.reshape(1, row_count)
    packed = pl.pallas_call(
        pack_kernel,
        in_specs=[hbm, hbm],
        out_specs=hbm,
        out_shape=pltpu.HBM((devices, slot_cap, features), jnp.bfloat16),
        scratch_shapes=[
            pltpu.VMEM((1, row_count), jnp.int32),
            pltpu.VMEM((row_count, features), jnp.bfloat16),
            pltpu.VMEM((devices, slot_cap, features), jnp.bfloat16),
            pltpu.SemaphoreType.DMA((copies,)),
        ],
        compiler_params=pltpu.CompilerParams(vmem_limit_bytes=VMEM_LIMIT),
        name="pack",
    )(*in_hbm(route_row, activations))
    arrived = lax.all_to_all(packed, AXES, split_axis=0, concat_axis=0, tiled=True)
    (outgoing, rows, latents, backward, preact_grad, bias_grad, logit_grad) = pl.pallas_call(
        expert_kernel,
        in_specs=[local, local, local, local, local, hbm],
        out_specs=(hbm,) * 5 + (local,) * 2,
        out_shape=(
            pltpu.HBM((devices, slot_cap, wide), jnp.bfloat16),
            pltpu.HBM((count, features), jnp.bfloat16),
            pltpu.HBM((count, latent_count), jnp.bfloat16),
            pltpu.HBM((count, features), jnp.bfloat16),
            pltpu.HBM((count, latent_count), jnp.bfloat16),
            jax.ShapeDtypeStruct((1, latent_count), jnp.float32),
            jax.ShapeDtypeStruct((count, 1), jnp.float32),
        ),
        scratch_shapes=[
            pltpu.VMEM((count, features), jnp.bfloat16),
            pltpu.VMEM((count, latent_count), jnp.bfloat16),
            pltpu.VMEM((count, features), jnp.bfloat16),
            pltpu.VMEM((count, latent_count), jnp.bfloat16),
            pltpu.VMEM((count, features), jnp.bfloat16),
            pltpu.VMEM((latent_count, features), jnp.bfloat16),
            pltpu.VMEM((devices, slot_cap, wide), jnp.bfloat16),
            pltpu.VMEM((count, latent_count), jnp.float32),
            pltpu.SemaphoreType.DMA((1 + PARTS + TAIL_COPIES,)),
            pltpu.SemaphoreType.DMA((4,)),
        ],
        compiler_params=pltpu.CompilerParams(vmem_limit_bytes=VMEM_LIMIT),
        name="expert",
    )(
        arrived,
        centre_bias[None],
        router,
        encoder[0],
        enc_bias,
        *in_hbm(decoder[0]),
    )
    returned = lax.all_to_all(outgoing, AXES, split_axis=0, concat_axis=0, tiled=True)
    router_grad = jnp.dot(
        logit_grad.astype(jnp.bfloat16).T, rows, preferred_element_type=jnp.float32
    )
    router_new = adam_update(router, router_grad, router_first, router_second)
    bias_new = adam_update(enc_bias, bias_grad, enc_bias_first, enc_bias_second)
    matrices = (
        encoder[0], encoder_first[0], encoder_second[0],
        decoder[0], decoder_first[0], decoder_second[0],
    )
    operands = (rows, preact_grad, latents, backward) + matrices
    pieces = 3 * (len(column_blocks(features)) + len(column_blocks(latent_count)))
    stepped = pl.pallas_call(
        step_kernel,
        in_specs=[local] + [hbm] * 10,
        out_specs=(hbm,) * 6,
        out_shape=tuple(pltpu.HBM(array.shape, array.dtype) for array in matrices),
        scratch_shapes=[pltpu.VMEM(array.shape, array.dtype) for array in operands + matrices]
        + [pltpu.SemaphoreType.DMA((pieces + 4,)), pltpu.SemaphoreType.DMA((pieces,))],
        compiler_params=pltpu.CompilerParams(vmem_limit_bytes=STEP_LIMIT),
        cost_estimate=pl.CostEstimate(
            flops=4 * count * features * latent_count,
            bytes_accessed=20 * features * latent_count,
            transcendentals=0,
        ),
        name="step",
    )(centre_bias[None], *in_hbm(*operands))
    encoder_new, decoder_new = stepped[:3], stepped[3:]
    taken = pl.pallas_call(
        taken_kernel,
        out_shape=jax.ShapeDtypeStruct((row_count, count), jnp.bfloat16),
        compiler_params=pltpu.CompilerParams(vmem_limit_bytes=VMEM_LIMIT),
        name="taken",
    )(route_row)
    recon, *centre_new = pl.pallas_call(
        unpack_kernel,
        out_shape=(jax.ShapeDtypeStruct((row_count, features), jnp.bfloat16),)
        + (jax.ShapeDtypeStruct((features,), jnp.float32),) * 3,
        compiler_params=params,
        name="unpack",
    )(taken, returned, centre_bias[None], centre_first[None], centre_second[None])
    return (
        recon,
        centre_new[0],
        centre_new[1],
        centre_new[2],
        router_new[0],
        router_new[1],
        router_new[2],
        encoder_new[0][None],
        bias_new[0],
        decoder_new[0][None],
        encoder_new[1][None],
        encoder_new[2][None],
        bias_new[1],
        bias_new[2],
        decoder_new[1][None],
        decoder_new[2][None],
    )


def solution(mesh):
    whole, rows, blocks = P(), P(AXES, None), P(AXES, None, None)
    return jax.shard_map(
        per_device,
        mesh=mesh,
        in_specs=(
            rows, rows, whole, whole, whole, rows, rows, rows, blocks, rows, blocks,
            blocks, blocks, rows, rows, blocks, blocks,
        ),
        out_specs=(
            rows, whole, whole, whole, rows, rows, rows, blocks, rows, blocks,
            blocks, blocks, rows, rows, blocks, blocks,
        ),
        check_vma=False,
    )
```

```python
import jax
import jax.numpy as jnp
from jax import lax
from jax.experimental import pallas as pl
from jax.experimental.pallas import tpu as pltpu
from jax.sharding import PartitionSpec as P

STEP = 10


learn_rate = 0.001
beta_one = 0.9
beta_two = 0.999
adam_eps = 1e-08
sparsity = 0.1

AXES = ("group", "member")
EMPTY_MARK = 64.0
EMPTY_LIMIT = 32.0
VMEM_LIMIT = 20 * 1024 * 1024
STEP_LIMIT = 36 * 1024 * 1024
PAIR = 2
NT = (((1,), (1,)), ((), ()))
TN = (((0,), (0,)), ((), ()))


def adam_update(weights_in, gradient, moment_one, moment_two):
    first_new = beta_one * moment_one + (1.0 - beta_one) * gradient
    second_new = beta_two * moment_two + (1.0 - beta_two) * gradient * gradient
    first_hat = first_new * (1.0 / (1.0 - beta_one**STEP))
    second_hat = second_new * (1.0 / (1.0 - beta_two**STEP))
    stepped = weights_in.astype(jnp.float32) - learn_rate * first_hat / (
        jnp.sqrt(second_hat) + adam_eps
    )
    return (stepped.astype(weights_in.dtype), first_new, second_new)


def slot_rows(ref, block, features):
    devices = ref.shape[0]
    halves = [
        ref[:, :, start + block.start : start + block.stop].reshape(
            devices * PAIR, block.stop - block.start
        )
        for start in (0, features)
    ]
    return jnp.concatenate(halves, axis=0)


def put_slot_rows(ref, block, features, values):
    devices = ref.shape[0]
    for i, start in enumerate((0, features)):
        ref[:, :, start + block.start : start + block.stop] = values[
            i * devices * PAIR : (i + 1) * devices * PAIR
        ].reshape(devices, PAIR, block.stop - block.start)


def slot_matrix(route_row, experts, slot_cap):
    rows = route_row.shape[1]
    onehot = lax.broadcasted_iota(jnp.int32, (experts, rows), 0) == route_row
    onehot = onehot.astype(jnp.float32)
    later = lax.broadcasted_iota(jnp.int32, (rows, rows), 0) < lax.broadcasted_iota(
        jnp.int32, (rows, rows), 1
    )
    before = jnp.dot(
        onehot.astype(jnp.bfloat16),
        later.astype(jnp.float32).astype(jnp.bfloat16),
        preferred_element_type=jnp.float32,
    )
    rank = jnp.sum(before * onehot, axis=0, keepdims=True).astype(jnp.int32)
    late = rank >= PAIR
    position = route_row * PAIR + jnp.where(late, rank - PAIR + experts * PAIR, rank)
    chosen = lax.broadcasted_iota(jnp.int32, (experts * slot_cap, rows), 0) == position
    return chosen.astype(jnp.float32)


def taken_kernel(route_ref, taken_ref):
    rows, slots = taken_ref.shape
    experts = lax.axis_size("group") * lax.axis_size("member")
    taken_ref[...] = slot_matrix(route_ref[...], experts, slots // experts).T.astype(jnp.bfloat16)


def pack_kernel(route_ref, rows_ref, packed_ref, route_vmem, rows_vmem, packed_vmem, sems):
    experts, features = packed_ref.shape[0], rows_ref.shape[1]
    slot_cap = packed_ref.shape[2] // features * PAIR
    fetch_route = pltpu.make_async_copy(route_ref, route_vmem, sems.at[1])
    fetch_route.start()
    fetch = pltpu.make_async_copy(rows_ref, rows_vmem, sems.at[0])
    fetch.start()
    fetch_route.wait()
    chosen = slot_matrix(route_vmem[...], experts, slot_cap)
    mark = (1.0 - jnp.sum(chosen, axis=1, keepdims=True)) * EMPTY_MARK
    chosen = chosen.astype(jnp.bfloat16)
    fetch.wait()
    copies = []
    ends = (3 * column_blocks(features)[0][1], features)
    for start, width in column_blocks(features):
        block = slice(start, start + width)
        part = jnp.dot(chosen, rows_vmem[:, block], preferred_element_type=jnp.float32)
        if start == 0:
            part = part + mark
        put_slot_rows(packed_vmem, block, features, part.astype(jnp.bfloat16))
        if start + width not in ends:
            continue
        ready = max((end for end in ends if end <= start), default=0)
        for shift in (0, features):
            place = slice(shift + ready, shift + start + width)
            copies.append(
                pltpu.make_async_copy(
                    packed_vmem.at[:, :, place], packed_ref.at[:, :, place], sems.at[2 + len(copies)]
                )
            )
            copies[-1].start()
    for copy in copies:
        copy.wait()


def unpack_kernel(
    taken_ref, returned_ref, centre_ref, first_ref, second_ref,
    recon_ref, new_centre_ref, new_first_ref, new_second_ref,
):
    features = recon_ref.shape[1]
    tail = returned_ref.shape[2] - 2 * features
    taken = taken_ref[...]
    for start, width in column_blocks(features):
        block = slice(start, start + width)
        recon_ref[:, block] = jnp.dot(
            taken, slot_rows(returned_ref, block, features), preferred_element_type=jnp.float32
        ).astype(jnp.bfloat16)
    total = jnp.sum(returned_ref[:, :, 2 * features :].astype(jnp.float32), axis=0)
    for i in range(PAIR):
        block = slice(i * tail, min((i + 1) * tail, features))
        width = block.stop - block.start
        updated = adam_update(
            centre_ref[:, block], total[i : i + 1, :width], first_ref[:, block], second_ref[:, block]
        )
        for value, target in zip(updated, (new_centre_ref, new_first_ref, new_second_ref)):
            target[block] = value.reshape(width)


def column_blocks(features, width=256):
    return [(start, min(width, features - start)) for start in range(0, features, width)]


def expert_kernel(
    arrived_ref,
    centre_ref,
    router_ref,
    encoder_ref,
    bias_ref,
    decoder_hbm,
    outgoing_hbm,
    rows_hbm,
    latents_hbm,
    backward_hbm,
    preact_grad_hbm,
    bias_grad_ref,
    logit_grad_ref,
    rows_ref,
    latents_ref,
    backward_ref,
    preact_grad_ref,
    centred_ref,
    decoder_ref,
    outgoing_ref,
    positive_ref,
    sems,
    side_sems,
):
    sources, features = arrived_ref.shape[0], rows_ref.shape[1]
    count = rows_ref.shape[0]
    tail = outgoing_ref.shape[2] - 2 * features
    fetch = pltpu.make_async_copy(decoder_hbm, decoder_ref, sems.at[0])
    fetch.start()
    copies = []

    def write_out(source, target, sem):
        copies.append(pltpu.make_async_copy(source, target, sem))
        copies[-1].start()

    centre = centre_ref[...]
    live = None
    for start, width in column_blocks(features):
        block = slice(start, start + width)
        wide_rows = slot_rows(arrived_ref, block, features)
        if live is None:
            live = wide_rows[:, 0:1].astype(jnp.float32) < EMPTY_LIMIT
            wide_rows = jnp.where(live, wide_rows.astype(jnp.float32), 0.0).astype(jnp.bfloat16)
        rows_ref[:, block] = wide_rows
        centred_ref[:, block] = (wide_rows.astype(jnp.float32) - centre[:, block]).astype(
            jnp.bfloat16
        )
    write_out(rows_ref, rows_hbm, side_sems.at[0])
    live_mask = live.astype(jnp.float32)
    logits = lax.dot_general(
        rows_ref[...],
        jnp.broadcast_to(router_ref[...], (8, features)),
        NT,
        preferred_element_type=jnp.float32,
    )[:, 0:1]
    gating = jax.nn.sigmoid(logits)
    for start, width in column_blocks(encoder_ref.shape[1]):
        block = slice(start, start + width)
        preact = (
            jnp.dot(centred_ref[...], encoder_ref[:, block], preferred_element_type=jnp.float32)
            + bias_ref[:, block]
        )
        positive = jnp.maximum(preact, 0.0)
        positive_ref[:, block] = positive * live_mask
        latents_ref[:, block] = (positive * positive).astype(jnp.bfloat16)
    write_out(latents_ref, latents_hbm, side_sems.at[1])
    fetch.wait()
    projected = jnp.zeros((count, 1), jnp.float32)
    error_sums = []
    for start, width in column_blocks(features):
        block = slice(start, start + width)
        ungated = jnp.dot(
            latents_ref[...], decoder_ref[:, block], preferred_element_type=jnp.float32
        )
        rebuilt = centre[:, block] + gating * ungated
        put_slot_rows(outgoing_ref, block, features, rebuilt.astype(jnp.bfloat16))
        errors = (rows_ref[:, block].astype(jnp.float32) - rebuilt) * live_mask
        backward_ref[:, block] = (-gating * errors).astype(jnp.bfloat16)
        projected = projected + jnp.sum(errors * ungated, axis=1, keepdims=True)
        error_sums.append(jnp.sum(errors, axis=0, keepdims=True))
    body = slice(0, 2 * features)
    write_out(outgoing_ref.at[:, :, body], outgoing_hbm.at[:, :, body], sems.at[1])
    write_out(backward_ref, backward_hbm, side_sems.at[2])
    logit_grad_ref[...] = -projected * gating * (1.0 - gating)
    bias_grads = []
    for start, width in column_blocks(encoder_ref.shape[1]):
        block = slice(start, start + width)
        latent_grad = lax.dot_general(
            backward_ref[...], decoder_ref[block, :], NT, preferred_element_type=jnp.float32
        )
        preact_grad = ((latent_grad + sparsity) * 2.0 * positive_ref[:, block]).astype(jnp.bfloat16)
        preact_grad_ref[:, block] = preact_grad
        bias_grads.append(jnp.sum(preact_grad.astype(jnp.float32), axis=0, keepdims=True))
    write_out(preact_grad_ref, preact_grad_hbm, side_sems.at[3])
    bias_grad = jnp.concatenate(bias_grads, axis=1)
    bias_grad_ref[...] = bias_grad
    high = bias_grad.astype(jnp.bfloat16).astype(jnp.float32)
    middle = (bias_grad - high).astype(jnp.bfloat16).astype(jnp.float32)
    low = bias_grad - high - middle
    row = lax.broadcasted_iota(jnp.int32, (8, 1), 0)
    terms = jnp.where(row == 0, high, jnp.where(row == 1, middle, jnp.where(row == 2, low, 0.0)))
    passed = jnp.sum(
        lax.dot_general(
            terms.astype(jnp.bfloat16), encoder_ref[...], NT, preferred_element_type=jnp.float32
        ),
        axis=0,
        keepdims=True,
    )
    centre_part = -jnp.concatenate(error_sums, axis=1) - passed
    spare = jnp.zeros((1, PAIR * tail - features), jnp.float32)
    padded = jnp.concatenate([centre_part, spare], axis=1)
    pieces = [padded[:, i * tail : (i + 1) * tail] for i in range(PAIR)]
    outgoing_ref[:, :, 2 * features :] = jnp.broadcast_to(
        jnp.concatenate(pieces, axis=0).astype(jnp.bfloat16)[None], (sources, PAIR, tail)
    )
    write_out(
        outgoing_ref.at[:, :, 2 * features :], outgoing_hbm.at[:, :, 2 * features :], sems.at[0]
    )
    for copy in copies:
        copy.wait()


def step_kernel(centre_ref, *refs):
    sources, targets = refs[:10], refs[10:16]
    arrived, made, (in_sems, out_sems) = refs[16:26], refs[26:32], refs[32:]
    rows, preact_grad, latents, backward = arrived[:4]
    plan = (
        (rows, preact_grad, (0, 1), (4, 5, 6), (0, 1, 2)),
        (latents, backward, (2, 3), (7, 8, 9), (3, 4, 5)),
    )
    fetches, started = [], 0
    for left, right, whole, state, _ in plan:
        waits = []
        for i in whole:
            waits.append(pltpu.make_async_copy(sources[i], arrived[i], in_sems.at[started]))
            started += 1
        for start, width in column_blocks(left.shape[1]):
            block = slice(start, start + width)
            for i in state:
                waits.append(
                    pltpu.make_async_copy(
                        sources[i].at[block, :], arrived[i].at[block, :], in_sems.at[started]
                    )
                )
                started += 1
            fetches.append(waits)
            waits = []
    for waits in fetches:
        for copy in waits:
            copy.start()
    copies = []
    fetched = iter(fetches)
    for left, right, _, state, made_here in plan:
        weights, first, second = (arrived[i] for i in state)
        for start, width in column_blocks(left.shape[1]):
            block = slice(start, start + width)
            for copy in next(fetched):
                copy.wait()
            turned = left[:, block]
            if left is rows:
                turned = (turned.astype(jnp.float32) - centre_ref[:, block]).astype(jnp.bfloat16)
            gradient = lax.dot_general(turned, right[...], TN, preferred_element_type=jnp.float32)
            updated = adam_update(weights[block, :], gradient, first[block, :], second[block, :])
            for value, i in zip(updated, made_here):
                made[i][block, :] = value
                copies.append(
                    pltpu.make_async_copy(
                        made[i].at[block, :], targets[i].at[block, :], out_sems.at[len(copies)]
                    )
                )
                copies[-1].start()
    for copy in copies:
        copy.wait()


def in_hbm(*arrays):
    return [pltpu.with_memory_space_constraint(array, pltpu.HBM) for array in arrays]


def per_device(
    activations,
    routes,
    centre_bias,
    centre_first,
    centre_second,
    router,
    router_first,
    router_second,
    encoder,
    enc_bias,
    decoder,
    encoder_first,
    encoder_second,
    enc_bias_first,
    enc_bias_second,
    decoder_first,
    decoder_second,
):
    devices = lax.axis_size("group") * lax.axis_size("member")
    row_count, features = activations.shape
    latent_count = encoder.shape[2]
    slot_cap = 2 * row_count // devices
    count = devices * slot_cap
    wide = 2 * features + -(-features // (128 * PAIR)) * 128
    params = pltpu.CompilerParams(vmem_limit_bytes=VMEM_LIMIT)
    hbm = pl.BlockSpec(memory_space=pltpu.HBM)
    local = pl.BlockSpec(memory_space=pltpu.VMEM)
    copies = 2 * len(column_blocks(features)) + 2
    route_row = routes.reshape(1, row_count)
    packed = pl.pallas_call(
        pack_kernel,
        in_specs=[hbm, hbm],
        out_specs=hbm,
        out_shape=pltpu.HBM((devices, PAIR, 2 * features), jnp.bfloat16),
        scratch_shapes=[
            pltpu.VMEM((1, row_count), jnp.int32),
            pltpu.VMEM((row_count, features), jnp.bfloat16),
            pltpu.VMEM((devices, PAIR, 2 * features), jnp.bfloat16),
            pltpu.SemaphoreType.DMA((copies,)),
        ],
        compiler_params=pltpu.CompilerParams(vmem_limit_bytes=VMEM_LIMIT),
        name="pack",
    )(*in_hbm(route_row, activations))
    arrived = lax.all_to_all(packed, AXES, split_axis=0, concat_axis=0, tiled=True)
    (outgoing, rows, latents, backward, preact_grad, bias_grad, logit_grad) = pl.pallas_call(
        expert_kernel,
        in_specs=[local, local, local, local, local, hbm],
        out_specs=(hbm,) * 5 + (local,) * 2,
        out_shape=(
            pltpu.HBM((devices, PAIR, wide), jnp.bfloat16),
            pltpu.HBM((count, features), jnp.bfloat16),
            pltpu.HBM((count, latent_count), jnp.bfloat16),
            pltpu.HBM((count, features), jnp.bfloat16),
            pltpu.HBM((count, latent_count), jnp.bfloat16),
            jax.ShapeDtypeStruct((1, latent_count), jnp.float32),
            jax.ShapeDtypeStruct((count, 1), jnp.float32),
        ),
        scratch_shapes=[
            pltpu.VMEM((count, features), jnp.bfloat16),
            pltpu.VMEM((count, latent_count), jnp.bfloat16),
            pltpu.VMEM((count, features), jnp.bfloat16),
            pltpu.VMEM((count, latent_count), jnp.bfloat16),
            pltpu.VMEM((count, features), jnp.bfloat16),
            pltpu.VMEM((latent_count, features), jnp.bfloat16),
            pltpu.VMEM((devices, PAIR, wide), jnp.bfloat16),
            pltpu.VMEM((count, latent_count), jnp.float32),
            pltpu.SemaphoreType.DMA((copies,)),
            pltpu.SemaphoreType.DMA((4,)),
        ],
        compiler_params=pltpu.CompilerParams(vmem_limit_bytes=VMEM_LIMIT),
        name="expert",
    )(
        arrived,
        centre_bias[None],
        router,
        encoder[0],
        enc_bias,
        *in_hbm(decoder[0]),
    )
    returned = lax.all_to_all(outgoing, AXES, split_axis=0, concat_axis=0, tiled=True)
    router_grad = jnp.dot(
        logit_grad.astype(jnp.bfloat16).T, rows, preferred_element_type=jnp.float32
    )
    router_new = adam_update(router, router_grad, router_first, router_second)
    bias_new = adam_update(enc_bias, bias_grad, enc_bias_first, enc_bias_second)
    matrices = (
        encoder[0], encoder_first[0], encoder_second[0],
        decoder[0], decoder_first[0], decoder_second[0],
    )
    operands = (rows, preact_grad, latents, backward) + matrices
    pieces = 3 * (len(column_blocks(features)) + len(column_blocks(latent_count)))
    stepped = pl.pallas_call(
        step_kernel,
        in_specs=[local] + [hbm] * 10,
        out_specs=(hbm,) * 6,
        out_shape=tuple(pltpu.HBM(array.shape, array.dtype) for array in matrices),
        scratch_shapes=[pltpu.VMEM(array.shape, array.dtype) for array in operands + matrices]
        + [pltpu.SemaphoreType.DMA((pieces + 4,)), pltpu.SemaphoreType.DMA((pieces,))],
        compiler_params=pltpu.CompilerParams(vmem_limit_bytes=STEP_LIMIT),
        cost_estimate=pl.CostEstimate(
            flops=4 * count * features * latent_count,
            bytes_accessed=20 * features * latent_count,
            transcendentals=0,
        ),
        name="step",
    )(centre_bias[None], *in_hbm(*operands))
    encoder_new, decoder_new = stepped[:3], stepped[3:]
    taken = pl.pallas_call(
        taken_kernel,
        out_shape=jax.ShapeDtypeStruct((row_count, count), jnp.bfloat16),
        compiler_params=pltpu.CompilerParams(vmem_limit_bytes=VMEM_LIMIT),
        name="taken",
    )(route_row)
    recon, *centre_new = pl.pallas_call(
        unpack_kernel,
        out_shape=(jax.ShapeDtypeStruct((row_count, features), jnp.bfloat16),)
        + (jax.ShapeDtypeStruct((features,), jnp.float32),) * 3,
        compiler_params=params,
        name="unpack",
    )(taken, returned, centre_bias[None], centre_first[None], centre_second[None])
    return (
        recon,
        centre_new[0],
        centre_new[1],
        centre_new[2],
        router_new[0],
        router_new[1],
        router_new[2],
        encoder_new[0][None],
        bias_new[0],
        decoder_new[0][None],
        encoder_new[1][None],
        encoder_new[2][None],
        bias_new[1],
        bias_new[2],
        decoder_new[1][None],
        decoder_new[2][None],
    )


def solution(mesh):
    whole, rows, blocks = P(), P(AXES, None), P(AXES, None, None)
    return jax.shard_map(
        per_device,
        mesh=mesh,
        in_specs=(
            rows, rows, whole, whole, whole, rows, rows, rows, blocks, rows, blocks,
            blocks, blocks, rows, rows, blocks, blocks,
        ),
        out_specs=(
            rows, whole, whole, whole, rows, rows, rows, blocks, rows, blocks,
            blocks, blocks, rows, rows, blocks, blocks,
        ),
        check_vma=False,
    )
```
